32 devices in a mesh: row: 4 (over x, core), col: 8 (over z, y).
Axes of the slice: x: 2, y: 2, z: 4, core: 2. Of those that a mesh axis runs over, the one named last changes fastest.
Arguments:
- features: bfloat16 [2048, 256], P(('row', 'col')), may hold values from -6 to 6
- adj_tiles: bfloat16 [4, 8, 3, 128, 128], P('row', 'col'), may hold values from -0.3125 to 0.3125
- tile_coord: int32 [4, 8, 3], P('row', 'col'), may hold values from 0 to 7, as said below
- tile_count: int32 [4, 8], P('row', 'col'), may hold values from 1 to 3, as said below
- weight: bfloat16 [256, 256], replicated, may hold values from -0.375 to 0.375
Outputs:
- out: bfloat16 [2048, 256], P(('col', 'row'))
The draws below stay inside these ranges and needn't reach their ends.
Inputs may be any that keep to these rules, and one draw needn't show every extreme that they name: `tile_coord`: each entry is t * 4 + s for a target tile t and a source tile s; within one device's list all entries differ. `tile_count`: slots from this number on are not part of the adjacency.
All inputs are finite; a program needn't handle non-finite values.
Results may differ from the reference program's by a relative error of at most 0.0049.
Values may be sent and summed in bfloat16 or wider, within the bound.
A program may use at most 128 MiB of HBM per device.

```python
import jax
import jax.numpy as jnp
from jax import lax

F = 256
TILE = 128
TGT_TILES = 2
SRC_TILES = 4
SLOTS = 3
NODES = 2048
N_ROW = 4
N_COL = 8


def draw_tile_coord(key, part):
    keys = jax.random.split(key, N_ROW * N_COL)

    def one_device(single):
        return jax.random.permutation(single, TGT_TILES * SRC_TILES)[:SLOTS].astype(jnp.int32)
    return jax.vmap(one_device)(keys).reshape(N_ROW, N_COL, SLOTS)


def draw_tile_count(key, part):
    total = N_ROW * N_COL
    counts = jax.random.randint(key, (total,), 1, SLOTS + 1).astype(jnp.int32)
    first = jax.random.randint(jax.random.fold_in(key, 11), (), 0, total)
    counts = counts.at[first].set(SLOTS)
    counts = counts.at[(first + 1) % total].set(1)
    return counts.reshape(N_ROW, N_COL)


def steps_of(own_key, dims, cuts, least, high):
    loudness, own = 1.0, jax.random.fold_in(own_key, 6)
    for axis_at, shards_of in cuts:
        draws = jnp.exp(jax.random.uniform(jax.random.fold_in(own, axis_at), (shards_of,), jnp.float32, least / len(cuts), high / len(cuts)))
        loudness = loudness * jnp.repeat(draws, dims[axis_at] // shards_of).reshape([-1 if axis == axis_at else 1 for axis in range(len(dims))])
    return loudness


def centred(stream_key, shape, deviation, reach, shards=(), kind=jnp.bfloat16):
    values = jax.random.normal(stream_key, shape, jnp.float32) * deviation
    if len(shards) > 0:
        values = steps_of(stream_key, shape, shards, -0.22, 0.18) * values
    return jnp.clip(values, min=-reach, max=reach).astype(kind)


def setup_inputs(seed: int = 0) -> dict:
    seeds = jax.random.split(jax.random.key(seed), 6)
    features = centred(seeds[0], (NODES, F), 1.0, 6.0, ((0, 32),))
    adj_tiles = centred(seeds[1], (N_ROW, N_COL, SLOTS, TILE, TILE), (max(1, SLOTS * N_ROW * TILE // (2 * TGT_TILES))) ** -0.5, 0.3125, ((0, 4), (1, 8)))
    tile_coord = draw_tile_coord(jax.random.fold_in(seeds[5], 71), 0)
    tile_count = draw_tile_count(jax.random.fold_in(seeds[5], 71), 0)
    weight = centred(seeds[4], (F, F), F ** -0.5, 0.375)
    return dict(features=features, adj_tiles=adj_tiles, tile_coord=tile_coord, tile_count=tile_count, weight=weight)


def device_partial(source_tiles, tile_vals, coord_list, live_count):
    live_mask = (jnp.arange(SLOTS) < live_count).astype(jnp.float32)
    target = coord_list // SRC_TILES
    source = coord_list % SRC_TILES
    feat_rows = source_tiles[source]
    products = jnp.einsum("kij,kjf->kif", tile_vals.astype(jnp.float32), feat_rows, precision=lax.Precision.HIGHEST)
    select = (target[:, None] == jnp.arange(TGT_TILES)[None, :]).astype(jnp.float32) * live_mask[:, None]
    partial_value = jnp.einsum("kt,kif->tif", select, products, precision=lax.Precision.HIGHEST)
    return partial_value.reshape(TGT_TILES * TILE, F)


def reference(features, adj_tiles, tile_coord, tile_count, weight):
    grouped = features.reshape(N_ROW, SRC_TILES, TILE, F)

    def per_row(total, inputs):
        row_feats, row_tiles, row_coords, row_counts = inputs
        source_tiles = row_feats.astype(jnp.float32)
        parts = lax.map(lambda item: device_partial(source_tiles, item[0], item[1], item[2]), (row_tiles, row_coords, row_counts))
        return total + parts, None

    start = jnp.zeros((N_COL, TGT_TILES * TILE, F), jnp.float32)
    total, unused = lax.scan(per_row, start, (grouped, adj_tiles, tile_coord, tile_count))
    hidden = total.reshape(NODES, F).astype(jnp.bfloat16)
    mixed = jnp.dot(hidden, weight, preferred_element_type=jnp.float32)
    return jax.nn.relu(mixed).astype(jnp.bfloat16)
```

```python
import functools

import jax
import jax.numpy as jnp
from jax import lax
from jax.experimental import pallas as pl
from jax.experimental.pallas import tpu as pltpu
from jax.sharding import PartitionSpec as P

MESH = pl.DeviceIdType.MESH
F32 = jnp.float32
BF16 = jnp.bfloat16


def kernel(
    n_row, n_z, n_y,
    x_ref, adj_ref, coord_ref, count_ref, w_ref, out_ref,
    feats, adj, weight, dense, total, stage, parts,
    own_sem, adj_sem, weight_sem, z_send, z_recv, y_send, y_recv, row_send, row_recv,
):
    row, col = lax.axis_index("row"), lax.axis_index("col")
    z, y = col // n_y, col % n_y
    slots, tile = adj_ref.shape[2], adj_ref.shape[3]
    rows = x_ref.shape[0]
    n_tgt = n_row * rows // tile
    n_src = n_z * n_y * rows // tile

    def piece(z_at, y_at):
        return feats.at[pl.ds(pl.multiple_of((z_at * n_y + y_at) * rows, rows), rows)]

    def z_peer(d):
        return {"col": lax.rem(z + d, n_z) * n_y + y}

    def y_peer(e):
        return {"col": z * n_y + lax.rem(y + e, n_y)}

    def row_peer(d):
        return {"row": lax.rem(row + d, n_row)}

    def back(at, d, n):
        return lax.rem(at + n - d, n)

    own_copy = pltpu.make_async_copy(x_ref, piece(z, y), own_sem)
    own_copy.start()
    adj_copy = pltpu.make_async_copy(adj_ref.at[0, 0], adj, adj_sem)
    adj_copy.start()
    weight_copy = pltpu.make_async_copy(w_ref, weight, weight_sem)
    weight_copy.start()

    barrier = pltpu.get_barrier_semaphore()
    peers = [z_peer(d) for d in range(1, n_z)]
    peers += [y_peer(e) for e in range(1, n_y)]
    peers += [row_peer(d) for d in range(1, n_row)]
    for peer in peers:
        pl.semaphore_signal(barrier, inc=1, device_id=peer, device_id_type=MESH)
    pl.semaphore_wait(barrier, len(peers))
    own_copy.wait()

    def z_copy(d, block):
        return pltpu.make_async_remote_copy(
            src_ref=block, dst_ref=block, send_sem=z_send.at[d], recv_sem=z_recv.at[d],
            device_id=z_peer(d), device_id_type=MESH,
        )

    def y_copy(e, d, block):
        return pltpu.make_async_remote_copy(
            src_ref=block, dst_ref=block, send_sem=y_send.at[e, d], recv_sem=y_recv.at[e, d],
            device_id=y_peer(e), device_id_type=MESH,
        )

    for d in range(1, n_z):
        z_copy(d, piece(z, y)).start()
    for e in range(1, n_y):
        y_copy(e, 0, piece(z, y)).start()

    adj_copy.wait()
    small = slots <= 8 and n_y * rows == tile

    def live(k):
        return jnp.where(k < count_ref[0, 0], coord_ref[0, 0, k], -1)

    if small:
        for s in range(n_src):
            for t in range(n_tgt):
                block = jnp.zeros((tile, tile), F32)
                for k in range(slots):
                    keep = jnp.where(live(k) == t * n_src + s, 1.0, 0.0).astype(F32)
                    block = block + adj[k].astype(F32) * keep
                dense[s, pl.ds(t * tile, tile), :] = block.astype(BF16)

    for d in range(n_z):
        z_from = back(z, d, n_z)
        if d > 0:
            z_copy(d, piece(z_from, y)).wait_recv()
            for e in range(1, n_y):
                y_copy(e, d, piece(z_from, y)).start()
    for d in range(n_z):
        z_from = back(z, d, n_z)
        for e in range(1, n_y):
            y_copy(e, d, piece(z_from, back(y, e, n_y))).wait_recv()
        if small:
            values = feats[pl.ds(pl.multiple_of(z_from * tile, tile), tile), :]
            product = jnp.dot(dense[z_from], values, preferred_element_type=F32)
            total[...] = product if d == 0 else total[...] + product

    if not small:
        total[...] = jnp.zeros_like(total)

        def add_slot(k, carry):
            at = live(k)
            source = jnp.where(at < 0, 0, lax.rem(at, n_src))
            values = feats[pl.ds(pl.multiple_of(source * tile, tile), tile), :]
            product = jnp.dot(adj[k], values, preferred_element_type=F32)
            for t in range(n_tgt):
                own = jnp.logical_and(at >= t * n_src, at < (t + 1) * n_src)
                total[pl.ds(t * tile, tile), :] += product * jnp.where(own, 1.0, 0.0).astype(F32)
            return carry

        lax.fori_loop(0, slots, add_slot, 0)

    def row_copy(d):
        return pltpu.make_async_remote_copy(
            src_ref=stage.at[d - 1], dst_ref=parts.at[d - 1],
            send_sem=row_send.at[d - 1], recv_sem=row_recv.at[d - 1],
            device_id=row_peer(d), device_id_type=MESH,
        )

    def block_of(r):
        return total[pl.ds(pl.multiple_of(r * rows, rows), rows), :]

    for d in range(1, n_row):
        stage[d - 1] = block_of(lax.rem(row + d, n_row)).astype(stage.dtype)
        row_copy(d).start()
    weight_copy.wait()
    hidden = block_of(row)
    for d in range(1, n_row):
        row_copy(d).wait_recv()
        hidden = hidden + parts[d - 1].astype(F32)
    mixed = jnp.dot(hidden.astype(BF16), weight[...], preferred_element_type=F32)
    out_ref[...] = jnp.maximum(mixed, 0.0).astype(out_ref.dtype)

    for d in range(1, n_z):
        z_copy(d, piece(z, y)).wait_send()
    for d in range(n_z):
        for e in range(1, n_y):
            y_copy(e, d, piece(back(z, d, n_z), y)).wait_send()
    for d in range(1, n_row):
        row_copy(d).wait_send()


def solution(mesh):
    n_row, n_col = mesh.shape["row"], mesh.shape["col"]
    n_y = max(1, n_row // 2)
    if n_col % n_y:
        n_y = 1
    n_z = n_col // n_y

    def on_device(features, adj_tiles, tile_coord, tile_count, weight):
        rows, width = features.shape
        slots, tile = adj_tiles.shape[2:4]
        n_tgt = n_row * rows // tile
        n_src = n_col * rows // tile
        small = slots <= 8 and n_y * rows == tile
        any_space = pl.BlockSpec(memory_space=pl.ANY)
        scalars = pl.BlockSpec(memory_space=pltpu.SMEM)
        dma = pltpu.SemaphoreType.DMA
        return pl.pallas_call(
            functools.partial(kernel, n_row, n_z, n_y),
            out_shape=jax.ShapeDtypeStruct((rows, weight.shape[1]), BF16),
            in_specs=[any_space, any_space, scalars, scalars, any_space],
            out_specs=pl.BlockSpec(memory_space=pltpu.VMEM),
            scratch_shapes=[
                pltpu.VMEM((n_col * rows, width), BF16),
                pltpu.VMEM((slots, tile, tile), BF16),
                pltpu.VMEM(weight.shape, BF16),
                pltpu.VMEM((n_src, n_tgt * tile, tile) if small else (1, 16, 128), BF16),
                pltpu.VMEM((n_tgt * tile, width), F32),
                pltpu.VMEM((n_row - 1, rows, width), BF16),
                pltpu.VMEM((n_row - 1, rows, width), BF16),
                dma, dma, dma,
                dma((n_z,)), dma((n_z,)),
                dma((max(n_y, 1), n_z)), dma((max(n_y, 1), n_z)),
                dma((n_row - 1,)), dma((n_row - 1,)),
            ],
            compiler_params=pltpu.CompilerParams(
                collective_id=0, has_side_effects=True, vmem_limit_bytes=32 * 2**20
            ),
        )(features, adj_tiles, tile_coord, tile_count, weight)

    return jax.shard_map(
        on_device,
        mesh=mesh,
        in_specs=(
            P(("row", "col"), None),
            P("row", "col", None, None, None),
            P("row", "col", None),
            P("row", "col"),
            P(),
        ),
        out_specs=P(("col", "row"), None),
        check_vma=False,
    )
```

```python
import functools

import jax
import jax.numpy as jnp
from jax import lax
from jax.experimental import pallas as pl
from jax.experimental.pallas import tpu as pltpu
from jax.sharding import PartitionSpec as P

MESH = pl.DeviceIdType.MESH
F32 = jnp.float32
BF16 = jnp.bfloat16


def kernel(
    n_row, n_z, n_y,
    x_ref, adj_ref, coord_ref, count_ref, w_ref, out_ref,
    feats, adj, weight, coord, count, dense, total, stage, parts,
    int_sems, own_sem, adj_sem, weight_sem, z_send, z_recv, y_send, y_recv, row_send, row_recv,
):
    row, col = lax.axis_index("row"), lax.axis_index("col")
    z, y = col // n_y, col % n_y
    slots, tile = adj_ref.shape[2], adj_ref.shape[3]
    rows = x_ref.shape[0]
    n_tgt = n_row * rows // tile
    n_src = n_z * n_y * rows // tile

    def piece(z_at, y_at):
        return feats.at[pl.ds(pl.multiple_of((z_at * n_y + y_at) * rows, rows), rows)]

    def z_peer(d):
        return {"col": lax.rem(z + d, n_z) * n_y + y}

    def y_peer(e):
        return {"col": z * n_y + lax.rem(y + e, n_y)}

    def row_peer(d):
        return {"row": lax.rem(row + d, n_row)}

    def back(at, d, n):
        return lax.rem(at + n - d, n)

    own_copy = pltpu.make_async_copy(x_ref, piece(z, y), own_sem)
    own_copy.start()
    coord_copy = pltpu.make_async_copy(coord_ref, coord, int_sems.at[0])
    coord_copy.start()
    count_copy = pltpu.make_async_copy(count_ref, count, int_sems.at[1])
    count_copy.start()
    adj_copy = pltpu.make_async_copy(adj_ref.at[0, 0], adj, adj_sem)
    adj_copy.start()
    weight_copy = pltpu.make_async_copy(w_ref, weight, weight_sem)
    weight_copy.start()

    barrier = pltpu.get_barrier_semaphore()
    peers = [z_peer(d) for d in range(1, n_z)]
    peers += [y_peer(e) for e in range(1, n_y)]
    peers += [row_peer(d) for d in range(1, n_row)]
    for peer in peers:
        pl.semaphore_signal(barrier, inc=1, device_id=peer, device_id_type=MESH)
    pl.semaphore_wait(barrier, len(peers))
    own_copy.wait()

    def z_copy(d, block):
        return pltpu.make_async_remote_copy(
            src_ref=block, dst_ref=block, send_sem=z_send.at[d], recv_sem=z_recv.at[d],
            device_id=z_peer(d), device_id_type=MESH,
        )

    def y_copy(e, d, block):
        return pltpu.make_async_remote_copy(
            src_ref=block, dst_ref=block, send_sem=y_send.at[e, d], recv_sem=y_recv.at[e, d],
            device_id=y_peer(e), device_id_type=MESH,
        )

    for d in range(1, n_z):
        z_copy(d, piece(z, y)).start()
    for e in range(1, n_y):
        y_copy(e, 0, piece(z, y)).start()

    coord_copy.wait()
    count_copy.wait()
    adj_copy.wait()
    small = slots <= 8 and n_y * rows == tile

    def live(k):
        return jnp.where(k < count[0, 0], coord[0, 0, k], -1)

    if small:
        for s in range(n_src):
            for t in range(n_tgt):
                block = jnp.zeros((tile, tile), F32)
                for k in range(slots):
                    keep = jnp.where(live(k) == t * n_src + s, 1.0, 0.0).astype(F32)
                    block = block + adj[k].astype(F32) * keep
                dense[s, pl.ds(t * tile, tile), :] = block.astype(BF16)

    for d in range(n_z):
        z_from = back(z, d, n_z)
        if d > 0:
            z_copy(d, piece(z_from, y)).wait_recv()
            for e in range(1, n_y):
                y_copy(e, d, piece(z_from, y)).start()
    for d in range(n_z):
        z_from = back(z, d, n_z)
        for e in range(1, n_y):
            y_copy(e, d, piece(z_from, back(y, e, n_y))).wait_recv()
        if small:
            values = feats[pl.ds(pl.multiple_of(z_from * tile, tile), tile), :]
            product = jnp.dot(dense[z_from], values, preferred_element_type=F32)
            total[...] = product if d == 0 else total[...] + product

    if not small:
        total[...] = jnp.zeros_like(total)

        def add_slot(k, carry):
            at = live(k)
            source = jnp.where(at < 0, 0, lax.rem(at, n_src))
            values = feats[pl.ds(pl.multiple_of(source * tile, tile), tile), :]
            product = jnp.dot(adj[k], values, preferred_element_type=F32)
            for t in range(n_tgt):
                own = jnp.logical_and(at >= t * n_src, at < (t + 1) * n_src)
                total[pl.ds(t * tile, tile), :] += product * jnp.where(own, 1.0, 0.0).astype(F32)
            return carry

        lax.fori_loop(0, slots, add_slot, 0)

    def row_copy(d):
        return pltpu.make_async_remote_copy(
            src_ref=stage.at[d - 1], dst_ref=parts.at[d - 1],
            send_sem=row_send.at[d - 1], recv_sem=row_recv.at[d - 1],
            device_id=row_peer(d), device_id_type=MESH,
        )

    def block_of(r):
        return total[pl.ds(pl.multiple_of(r * rows, rows), rows), :]

    for d in range(1, n_row):
        stage[d - 1] = block_of(lax.rem(row + d, n_row)).astype(stage.dtype)
        row_copy(d).start()
    weight_copy.wait()
    hidden = block_of(row)
    for d in range(1, n_row):
        row_copy(d).wait_recv()
        hidden = hidden + parts[d - 1].astype(F32)
    mixed = jnp.dot(hidden.astype(BF16), weight[...], preferred_element_type=F32)
    out_ref[...] = jnp.maximum(mixed, 0.0).astype(out_ref.dtype)

    for d in range(1, n_z):
        z_copy(d, piece(z, y)).wait_send()
    for d in range(n_z):
        for e in range(1, n_y):
            y_copy(e, d, piece(back(z, d, n_z), y)).wait_send()
    for d in range(1, n_row):
        row_copy(d).wait_send()


def solution(mesh):
    n_row, n_col = mesh.shape["row"], mesh.shape["col"]
    n_y = max(1, n_row // 2)
    if n_col % n_y:
        n_y = 1
    n_z = n_col // n_y

    def on_device(features, adj_tiles, tile_coord, tile_count, weight):
        rows, width = features.shape
        slots, tile = adj_tiles.shape[2:4]
        n_tgt = n_row * rows // tile
        n_src = n_col * rows // tile
        small = slots <= 8 and n_y * rows == tile
        in_hbm = pl.BlockSpec(memory_space=pltpu.HBM)
        dma = pltpu.SemaphoreType.DMA
        return pl.pallas_call(
            functools.partial(kernel, n_row, n_z, n_y),
            out_shape=jax.ShapeDtypeStruct((rows, weight.shape[1]), BF16),
            in_specs=[in_hbm] * 5,
            out_specs=pl.BlockSpec(memory_space=pltpu.VMEM),
            scratch_shapes=[
                pltpu.VMEM((n_col * rows, width), BF16),
                pltpu.VMEM((slots, tile, tile), BF16),
                pltpu.VMEM(weight.shape, BF16),
                pltpu.SMEM(tile_coord.shape, jnp.int32),
                pltpu.SMEM(tile_count.shape, jnp.int32),
                pltpu.VMEM((n_src, n_tgt * tile, tile) if small else (1, 16, 128), BF16),
                pltpu.VMEM((n_tgt * tile, width), F32),
                pltpu.VMEM((n_row - 1, rows, width), BF16),
                pltpu.VMEM((n_row - 1, rows, width), BF16),
                dma((2,)), dma, dma, dma,
                dma((n_z,)), dma((n_z,)),
                dma((max(n_y, 1), n_z)), dma((max(n_y, 1), n_z)),
                dma((n_row - 1,)), dma((n_row - 1,)),
            ],
            compiler_params=pltpu.CompilerParams(
                collective_id=0, has_side_effects=True, vmem_limit_bytes=64 * 2**20
            ),
        )(features, adj_tiles, tile_coord, tile_count, weight)

    return jax.shard_map(
        on_device,
        mesh=mesh,
        in_specs=(
            P(("row", "col"), None),
            P("row", "col", None, None, None),
            P("row", "col", None),
            P("row", "col"),
            P(),
        ),
        out_specs=P(("col", "row"), None),
        check_vma=False,
    )
```

```python
import functools

import jax
import jax.numpy as jnp
from jax import lax
from jax.experimental import pallas as pl
from jax.experimental.pallas import tpu as pltpu
from jax.sharding import PartitionSpec as P

MESH = pl.DeviceIdType.MESH
F32 = jnp.float32
BF16 = jnp.bfloat16


def kernel(
    n_row, n_z, n_y,
    x_ref, adj_ref, coord_ref, count_ref, w_ref, out_ref,
    feats, adj, weight, coord, count, dense, total, stage, parts,
    int_sems, own_sems, adj_sem, weight_sem, z_send, z_recv, y_send, y_recv, row_send, row_recv,
):
    row, col = lax.axis_index("row"), lax.axis_index("col")
    z, y = col // n_y, col % n_y
    slots, tile = adj_ref.shape[2], adj_ref.shape[3]
    rows = x_ref.shape[0]
    halves, _, width = feats.shape
    n_tgt = n_row * rows // tile
    n_src = n_z * n_y * rows // tile
    row_order = sorted(range(1, n_row), key=lambda d: d % 2)

    def piece(h, z_at, y_at):
        return feats.at[h, pl.ds(pl.multiple_of((z_at * n_y + y_at) * rows, rows), rows)]

    def z_peer(d):
        return {"col": lax.rem(z + d, n_z) * n_y + y}

    def y_peer(e):
        return {"col": z * n_y + lax.rem(y + e, n_y)}

    def row_peer(d):
        return {"row": lax.rem(row + d, n_row)}

    def back(at, d, n):
        return lax.rem(at + n - d, n)

    own_copies = [
        pltpu.make_async_copy(x_ref.at[:, pl.ds(h * width, width)], piece(h, z, y), own_sems.at[h])
        for h in range(halves)
    ]
    for copy in own_copies:
        copy.start()
    coord_copy = pltpu.make_async_copy(coord_ref, coord, int_sems.at[0])
    coord_copy.start()
    count_copy = pltpu.make_async_copy(count_ref, count, int_sems.at[1])
    count_copy.start()
    adj_copy = pltpu.make_async_copy(adj_ref.at[0, 0], adj, adj_sem)
    adj_copy.start()
    weight_copy = pltpu.make_async_copy(w_ref, weight, weight_sem)
    weight_copy.start()

    barrier = pltpu.get_barrier_semaphore()
    peers = [z_peer(d) for d in range(1, n_z)]
    peers += [y_peer(e) for e in range(1, n_y)]
    peers += [row_peer(d) for d in range(1, n_row)]
    for peer in peers:
        pl.semaphore_signal(barrier, inc=1, device_id=peer, device_id_type=MESH)
    pl.semaphore_wait(barrier, len(peers))

    def z_copy(h, d, block):
        return pltpu.make_async_remote_copy(
            src_ref=block, dst_ref=block, send_sem=z_send.at[h, d], recv_sem=z_recv.at[h, d],
            device_id=z_peer(d), device_id_type=MESH,
        )

    def y_copy(h, e, d, block):
        return pltpu.make_async_remote_copy(
            src_ref=block, dst_ref=block, send_sem=y_send.at[h, e, d], recv_sem=y_recv.at[h, e, d],
            device_id=y_peer(e), device_id_type=MESH,
        )

    for h in range(halves):
        own_copies[h].wait()
        for d in range(1, n_z):
            z_copy(h, d, piece(h, z, y)).start()
        for e in range(1, n_y):
            y_copy(h, e, 0, piece(h, z, y)).start()

    coord_copy.wait()
    count_copy.wait()
    adj_copy.wait()
    small = slots <= 8 and n_y * rows == tile

    def live(k):
        return jnp.where(k < count[0, 0], coord[0, 0, k], -1)

    if small:
        for s in range(n_src):
            for t in range(n_tgt):
                block = jnp.zeros((tile, tile), F32)
                for k in range(slots):
                    keep = jnp.where(live(k) == t * n_src + s, 1.0, 0.0).astype(F32)
                    block = block + adj[k].astype(F32) * keep
                dense[s, pl.ds(t * tile, tile), :] = block.astype(BF16)

    for h in range(halves):
        for d in range(1, n_z):
            block = piece(h, back(z, d, n_z), y)
            z_copy(h, d, block).wait_recv()
            for e in range(1, n_y):
                y_copy(h, e, d, block).start()

    def row_copy(h, d):
        return pltpu.make_async_remote_copy(
            src_ref=stage.at[h, d - 1], dst_ref=parts.at[h, d - 1],
            send_sem=row_send.at[h, d - 1], recv_sem=row_recv.at[h, d - 1],
            device_id=row_peer(d), device_id_type=MESH,
        )

    def block_of(h, r):
        return total[h, pl.ds(pl.multiple_of(r * rows, rows), rows), :]

    for h in range(halves):
        product = None
        for d in range(n_z):
            z_from = back(z, d, n_z)
            for e in range(1, n_y):
                y_copy(h, e, d, piece(h, z_from, back(y, e, n_y))).wait_recv()
            if small:
                values = feats[h, pl.ds(pl.multiple_of(z_from * tile, tile), tile), :]
                term = jnp.dot(dense[z_from], values, preferred_element_type=F32)
                product = term if d == 0 else product + term
        if small:
            total[h] = product
        else:
            total[h] = jnp.zeros(total.shape[1:], F32)

            def add_slot(k, carry):
                at = live(k)
                source = jnp.where(at < 0, 0, lax.rem(at, n_src))
                values = feats[h, pl.ds(pl.multiple_of(source * tile, tile), tile), :]
                term = jnp.dot(adj[k], values, preferred_element_type=F32)
                for t in range(n_tgt):
                    own = jnp.logical_and(at >= t * n_src, at < (t + 1) * n_src)
                    total[h, pl.ds(t * tile, tile), :] += term * jnp.where(own, 1.0, 0.0).astype(F32)
                return carry

            lax.fori_loop(0, slots, add_slot, 0)
        for d in row_order:
            stage[h, d - 1] = block_of(h, lax.rem(row + d, n_row)).astype(stage.dtype)
            row_copy(h, d).start()

    weight_copy.wait()
    mixed = None
    for h in range(halves):
        hidden = block_of(h, row)
        for d in reversed(row_order):
            row_copy(h, d).wait_recv()
            hidden = hidden + parts[h, d - 1].astype(F32)
        term = jnp.dot(
            hidden.astype(BF16), weight[pl.ds(h * width, width), :], preferred_element_type=F32
        )
        mixed = term if h == 0 else mixed + term
    out_ref[...] = jnp.maximum(mixed, 0.0).astype(out_ref.dtype)

    for h in range(halves):
        for d in range(1, n_z):
            z_copy(h, d, piece(h, z, y)).wait_send()
        for d in range(n_z):
            for e in range(1, n_y):
                y_copy(h, e, d, piece(h, back(z, d, n_z), y)).wait_send()
        for d in range(1, n_row):
            row_copy(h, d).wait_send()


def solution(mesh):
    n_row, n_col = mesh.shape["row"], mesh.shape["col"]
    n_y = max(1, n_row // 2)
    if n_col % n_y:
        n_y = 1
    n_z = n_col // n_y

    def on_device(features, adj_tiles, tile_coord, tile_count, weight):
        rows, width = features.shape
        slots, tile = adj_tiles.shape[2:4]
        n_tgt = n_row * rows // tile
        n_src = n_col * rows // tile
        small = slots <= 8 and n_y * rows == tile
        in_hbm = pl.BlockSpec(memory_space=pltpu.HBM)
        dma = pltpu.SemaphoreType.DMA
        halves = 2
        half = width // halves
        return pl.pallas_call(
            functools.partial(kernel, n_row, n_z, n_y),
            out_shape=jax.ShapeDtypeStruct((rows, weight.shape[1]), BF16),
            in_specs=[in_hbm] * 5,
            out_specs=pl.BlockSpec(memory_space=pltpu.VMEM),
            scratch_shapes=[
                pltpu.VMEM((halves, n_col * rows, half), BF16),
                pltpu.VMEM((slots, tile, tile), BF16),
                pltpu.VMEM(weight.shape, BF16),
                pltpu.SMEM(tile_coord.shape, jnp.int32),
                pltpu.SMEM(tile_count.shape, jnp.int32),
                pltpu.VMEM((n_src, n_tgt * tile, tile) if small else (1, 16, 128), BF16),
                pltpu.VMEM((halves, n_tgt * tile, half), F32),
                pltpu.VMEM((halves, n_row - 1, rows, half), BF16),
                pltpu.VMEM((halves, n_row - 1, rows, half), BF16),
                dma((2,)), dma((halves,)), dma, dma,
                dma((halves, n_z)), dma((halves, n_z)),
                dma((halves, n_y, n_z)), dma((halves, n_y, n_z)),
                dma((halves, n_row - 1)), dma((halves, n_row - 1)),
            ],
            compiler_params=pltpu.CompilerParams(
                collective_id=0, has_side_effects=True, vmem_limit_bytes=64 * 2**20
            ),
        )(features, adj_tiles, tile_coord, tile_count, weight)

    return jax.shard_map(
        on_device,
        mesh=mesh,
        in_specs=(
            P(("row", "col"), None),
            P("row", "col", None, None, None),
            P("row", "col", None),
            P("row", "col"),
            P(),
        ),
        out_specs=P(("col", "row"), None),
        check_vma=False,
    )
```

```python
import functools

import jax
import jax.numpy as jnp
from jax import lax
from jax.experimental import pallas as pl
from jax.experimental.pallas import tpu as pltpu
from jax.sharding import PartitionSpec as P

MESH = pl.DeviceIdType.MESH
F32 = jnp.float32
BF16 = jnp.bfloat16


def kernel(
    n_row, n_z, n_y,
    x_ref, adj_ref, coord_ref, count_ref, w_ref, out_ref,
    feats, adj, weight, coord, count, dense, total, stage, parts,
    int_sems, own_sems, adj_sem, weight_sem, z_send, z_recv, y_send, y_recv, row_send, row_recv,
):
    row, col = lax.axis_index("row"), lax.axis_index("col")
    z, y = col // n_y, col % n_y
    slots, tile = adj_ref.shape[2], adj_ref.shape[3]
    rows = x_ref.shape[0]
    halves, _, width = feats.shape
    n_tgt = n_row * rows // tile
    n_src = n_z * n_y * rows // tile
    row_order = sorted(range(1, n_row), key=lambda d: d % 2)

    def piece(h, z_at, y_at):
        return feats.at[h, pl.ds(pl.multiple_of((z_at * n_y + y_at) * rows, rows), rows)]

    def z_peer(d):
        return {"col": lax.rem(z + d, n_z) * n_y + y}

    def y_peer(e):
        return {"col": z * n_y + lax.rem(y + e, n_y)}

    def row_peer(d):
        return {"row": lax.rem(row + d, n_row)}

    def back(at, d, n):
        return lax.rem(at + n - d, n)

    own_copies = [
        pltpu.make_async_copy(x_ref.at[:, pl.ds(h * width, width)], piece(h, z, y), own_sems.at[h])
        for h in range(halves)
    ]
    for copy in own_copies:
        copy.start()
    coord_copy = pltpu.make_async_copy(coord_ref, coord, int_sems.at[0])
    coord_copy.start()
    count_copy = pltpu.make_async_copy(count_ref, count, int_sems.at[1])
    count_copy.start()
    adj_copy = pltpu.make_async_copy(adj_ref.at[0, 0], adj, adj_sem)
    adj_copy.start()
    weight_copy = pltpu.make_async_copy(w_ref, weight, weight_sem)
    weight_copy.start()

    barrier = pltpu.get_barrier_semaphore()
    peers = [z_peer(d) for d in range(1, n_z)]
    peers += [y_peer(e) for e in range(1, n_y)]
    peers += [row_peer(d) for d in range(1, n_row)]
    for peer in peers:
        pl.semaphore_signal(barrier, inc=1, device_id=peer, device_id_type=MESH)
    pl.semaphore_wait(barrier, len(peers))

    def z_copy(h, d, block):
        return pltpu.make_async_remote_copy(
            src_ref=block, dst_ref=block, send_sem=z_send.at[h, d], recv_sem=z_recv.at[h, d],
            device_id=z_peer(d), device_id_type=MESH,
        )

    def y_copy(h, e, d, block):
        return pltpu.make_async_remote_copy(
            src_ref=block, dst_ref=block, send_sem=y_send.at[h, e, d], recv_sem=y_recv.at[h, e, d],
            device_id=y_peer(e), device_id_type=MESH,
        )

    for h in range(halves):
        own_copies[h].wait()
        for d in range(1, n_z):
            z_copy(h, d, piece(h, z, y)).start()
        for e in range(1, n_y):
            y_copy(h, e, 0, piece(h, z, y)).start()

    coord_copy.wait()
    count_copy.wait()
    adj_copy.wait()
    small = slots <= 8 and n_y * rows == tile

    def live(k):
        return jnp.where(k < count[0, 0], coord[0, 0, k], -1)

    if small:
        for s in range(n_src):
            for t in range(n_tgt):
                block = jnp.zeros((tile, tile), F32)
                for k in range(slots):
                    keep = jnp.where(live(k) == t * n_src + s, 1.0, 0.0).astype(F32)
                    block = block + adj[k].astype(F32) * keep
                dense[s, pl.ds(t * tile, tile), :] = block.astype(BF16)

    for h in range(halves):
        for d in range(1, n_z):
            block = piece(h, back(z, d, n_z), y)
            z_copy(h, d, block).wait_recv()
            for e in range(1, n_y):
                y_copy(h, e, d, block).start()

    def row_copy(h, d):
        return pltpu.make_async_remote_copy(
            src_ref=stage.at[h, d - 1], dst_ref=parts.at[h, d - 1],
            send_sem=row_send.at[h, d - 1], recv_sem=row_recv.at[h, d - 1],
            device_id=row_peer(d), device_id_type=MESH,
        )

    def block_of(h, r):
        return total[h, pl.ds(pl.multiple_of(r * rows, rows), rows), :]

    for h in range(halves):
        product = None
        for d in range(n_z):
            z_from = back(z, d, n_z)
            for e in range(1, n_y):
                y_copy(h, e, d, piece(h, z_from, back(y, e, n_y))).wait_recv()
            if small:
                values = feats[h, pl.ds(pl.multiple_of(z_from * tile, tile), tile), :]
                term = jnp.dot(dense[z_from], values, preferred_element_type=F32)
                product = term if d == 0 else product + term
        if small:
            total[h] = product
        else:
            total[h] = jnp.zeros(total.shape[1:], F32)

            def add_slot(k, carry):
                at = live(k)
                source = jnp.where(at < 0, 0, lax.rem(at, n_src))
                values = feats[h, pl.ds(pl.multiple_of(source * tile, tile), tile), :]
                term = jnp.dot(adj[k], values, preferred_element_type=F32)
                for t in range(n_tgt):
                    own = jnp.logical_and(at >= t * n_src, at < (t + 1) * n_src)
                    total[h, pl.ds(t * tile, tile), :] += term * jnp.where(own, 1.0, 0.0).astype(F32)
                return carry

            lax.fori_loop(0, slots, add_slot, 0)
        for d in row_order:
            stage[h, d - 1] = block_of(h, lax.rem(row + d, n_row)).astype(stage.dtype)
            row_copy(h, d).start()

    weight_copy.wait()
    mixed = None
    for h in range(halves):
        hidden = block_of(h, row)
        for d in reversed(row_order):
            row_copy(h, d).wait_recv()
            hidden = hidden + parts[h, d - 1].astype(F32)
        term = jnp.dot(
            hidden.astype(BF16), weight[pl.ds(h * width, width), :], preferred_element_type=F32
        )
        mixed = term if h == 0 else mixed + term
    out_ref[...] = jnp.maximum(mixed, 0.0).astype(out_ref.dtype)

    for h in range(halves):
        for d in range(1, n_z):
            z_copy(h, d, piece(h, z, y)).wait_send()
        for d in range(n_z):
            for e in range(1, n_y):
                y_copy(h, e, d, piece(h, back(z, d, n_z), y)).wait_send()
        for d in range(1, n_row):
            row_copy(h, d).wait_send()


def pair_kernel(
    n_row, n_col,
    x_ref, adj_ref, coord_ref, count_ref, w_ref, out_ref,
    own, feats, adj, weight, coord, count, code, dense, total, stage, parts,
    int_sems, own_sems, adj_sem, weight_sem,
    pair_send, pair_recv, col_send, col_recv, row_send, row_recv,
):
    row, col = lax.axis_index("row"), lax.axis_index("col")
    side = col % 2
    pair = col + 1 - 2 * side
    slots, tile = adj_ref.shape[2], adj_ref.shape[3]
    rows, half = x_ref.shape[0], feats.shape[1]
    n_tgt, n_src = n_row * rows // tile, n_col * rows // tile
    targets = n_tgt * tile

    def piece(c):
        return feats.at[pl.ds(pl.multiple_of(c * rows, rows), rows)]

    def columns(h):
        return x_ref.at[:, pl.ds(pl.multiple_of(h * half, half), half)]

    coord_copy = pltpu.make_async_copy(coord_ref, coord, int_sems.at[0])
    count_copy = pltpu.make_async_copy(count_ref, count, int_sems.at[1])
    adj_copy = pltpu.make_async_copy(adj_ref.at[0, 0], adj.at[0], adj_sem)
    weight_copy = pltpu.make_async_copy(w_ref, weight, weight_sem)
    own_copies = [pltpu.make_async_copy(columns(h), own.at[h], own_sems.at[h]) for h in range(2)]
    own_copies.append(pltpu.make_async_copy(columns(side), piece(col), own_sems.at[2]))
    for copy in own_copies + [coord_copy, count_copy, adj_copy, weight_copy]:
        copy.start()

    row_peers = [(e, d) for d in range(n_row) for e in range(2) if e + d > 0]
    row_peers.sort(key=lambda ed: (ed[1] % 2, -ed[1]))

    def row_peer(e, d):
        return {"row": lax.rem(row + d, n_row), "col": pair if e else col}

    barrier = pltpu.get_barrier_semaphore()
    peers = [{"col": lax.rem(col + d, n_col)} for d in range(1, n_col)]
    peers += [row_peer(e, d) for e, d in row_peers if d > 0]
    for peer in peers:
        pl.semaphore_signal(barrier, inc=1, device_id=peer, device_id_type=MESH)
    pl.semaphore_wait(barrier, len(peers))

    pair_adj = pltpu.make_async_remote_copy(
        src_ref=adj_ref.at[0, 0], dst_ref=adj.at[1], send_sem=pair_send.at[0],
        recv_sem=pair_recv.at[0], device_id={"col": pair}, device_id_type=MESH,
    )
    pair_adj.start()
    for copy in own_copies:
        copy.wait()

    def col_copy(d):
        return pltpu.make_async_remote_copy(
            src_ref=own.at[lax.rem(side + d, 2)], dst_ref=piece(col), send_sem=col_send.at[d],
            recv_sem=col_recv.at[col], device_id={"col": lax.rem(col + d, n_col)},
            device_id_type=MESH,
        )

    for d in range(1, n_col):
        col_copy(d).start()

    coord_copy.wait()
    count_copy.wait()
    for k in range(slots):
        at = jnp.where(k < count[0, 0], coord[0, 0, k], -1)
        code[0, pl.ds(k, 1), :] = jnp.full((1, tile), at, jnp.int32)
    pair_code = pltpu.make_async_remote_copy(
        src_ref=code.at[0], dst_ref=code.at[1], send_sem=pair_send.at[1],
        recv_sem=pair_recv.at[1], device_id={"col": pair}, device_id_type=MESH,
    )
    pair_code.start()

    def spread(e):
        for s in range(n_src):
            for t in range(n_tgt):
                block = jnp.zeros((tile, tile), F32)
                for k in range(slots):
                    keep = jnp.where(code[e, pl.ds(k, 1), :] == t * n_src + s, 1.0, 0.0).astype(F32)
                    block = block + adj[e, k].astype(F32) * keep
                dense[s, pl.ds(e * targets + t * tile, tile), :] = block.astype(BF16)

    adj_copy.wait()
    spread(0)
    pair_adj.wait_recv()
    pair_code.wait_recv()
    spread(1)

    def arrived(c):
        pltpu.make_async_remote_copy(
            src_ref=own.at[0], dst_ref=piece(c), send_sem=col_send.at[0],
            recv_sem=col_recv.at[c], device_id={"col": pair}, device_id_type=MESH,
        ).wait_recv()

    product = None
    for q in range(n_src):
        s = lax.rem(col // 2 + q, n_src)
        if q == 0:
            arrived(pair)
        else:
            arrived(2 * s)
            arrived(2 * s + 1)
        values = feats[pl.ds(pl.multiple_of(s * tile, tile), tile), :]
        term = jnp.dot(dense[s], values, preferred_element_type=F32)
        product = term if q == 0 else product + term
    total[...] = product

    def row_copy(e, d):
        return pltpu.make_async_remote_copy(
            src_ref=stage.at[e, d], dst_ref=parts.at[e, d], send_sem=row_send.at[e, d],
            recv_sem=row_recv.at[e, d], device_id=row_peer(e, d), device_id_type=MESH,
        )

    def block_of(e, r):
        return total[pl.ds(pl.multiple_of(e * targets + r * rows, rows), rows), :]

    for e, d in row_peers:
        stage[e, d] = block_of(e, lax.rem(row + d, n_row)).astype(stage.dtype)
        row_copy(e, d).start()
    weight_copy.wait()
    hidden = [block_of(0, row), jnp.zeros((rows, half), F32)]
    for e, d in reversed(row_peers):
        row_copy(e, d).wait_recv()
        hidden[e] = hidden[e] + parts[e, d].astype(F32)

    def weight_rows(h):
        return weight[pl.ds(pl.multiple_of(h * half, half), half), :]

    mixed = jnp.dot(hidden[0].astype(BF16), weight_rows(side), preferred_element_type=F32)
    mixed += jnp.dot(hidden[1].astype(BF16), weight_rows(1 - side), preferred_element_type=F32)
    out_ref[...] = jnp.maximum(mixed, 0.0).astype(out_ref.dtype)

    pair_adj.wait_send()
    pair_code.wait_send()
    for d in range(1, n_col):
        col_copy(d).wait_send()
    for e, d in row_peers:
        row_copy(e, d).wait_send()


def pair_call(n_row, n_col, features, adj_tiles, tile_coord, tile_count, weight):
    rows, width = features.shape
    slots, tile = adj_tiles.shape[2:4]
    targets, n_src, half = n_row * rows, n_col * rows // tile, width // 2
    dma = pltpu.SemaphoreType.DMA
    return pl.pallas_call(
        functools.partial(pair_kernel, n_row, n_col),
        out_shape=jax.ShapeDtypeStruct((rows, weight.shape[1]), BF16),
        in_specs=[pl.BlockSpec(memory_space=pltpu.HBM)] * 5,
        out_specs=pl.BlockSpec(memory_space=pltpu.VMEM),
        scratch_shapes=[
            pltpu.VMEM((2, rows, half), BF16),
            pltpu.VMEM((n_col * rows, half), BF16),
            pltpu.VMEM((2, slots, tile, tile), BF16),
            pltpu.VMEM(weight.shape, BF16),
            pltpu.SMEM(tile_coord.shape, jnp.int32),
            pltpu.SMEM(tile_count.shape, jnp.int32),
            pltpu.VMEM((2, 8, tile), jnp.int32),
            pltpu.VMEM((n_src, 2 * targets, tile), BF16),
            pltpu.VMEM((2 * targets, half), F32),
            pltpu.VMEM((2, n_row, rows, half), BF16),
            pltpu.VMEM((2, n_row, rows, half), BF16),
            dma((2,)), dma((3,)), dma, dma,
            dma((2,)), dma((2,)),
            dma((n_col,)), dma((n_col,)),
            dma((2, n_row)), dma((2, n_row)),
        ],
        compiler_params=pltpu.CompilerParams(
            collective_id=0, has_side_effects=True, vmem_limit_bytes=64 * 2**20
        ),
    )(features, adj_tiles, tile_coord, tile_count, weight)


def solution(mesh):
    n_row, n_col = mesh.shape["row"], mesh.shape["col"]
    n_y = max(1, n_row // 2)
    if n_col % n_y:
        n_y = 1
    n_z = n_col // n_y

    def on_device(features, adj_tiles, tile_coord, tile_count, weight):
        rows, width = features.shape
        slots, tile = adj_tiles.shape[2:4]
        n_tgt = n_row * rows // tile
        n_src = n_col * rows // tile
        paired = slots <= 8 and 2 * rows == tile and width == 2 * tile and n_col % 2 == 0
        if paired:
            return pair_call(n_row, n_col, features, adj_tiles, tile_coord, tile_count, weight)
        small = slots <= 8 and n_y * rows == tile
        in_hbm = pl.BlockSpec(memory_space=pltpu.HBM)
        dma = pltpu.SemaphoreType.DMA
        halves = 2
        half = width // halves
        return pl.pallas_call(
            functools.partial(kernel, n_row, n_z, n_y),
            out_shape=jax.ShapeDtypeStruct((rows, weight.shape[1]), BF16),
            in_specs=[in_hbm] * 5,
            out_specs=pl.BlockSpec(memory_space=pltpu.VMEM),
            scratch_shapes=[
                pltpu.VMEM((halves, n_col * rows, half), BF16),
                pltpu.VMEM((slots, tile, tile), BF16),
                pltpu.VMEM(weight.shape, BF16),
                pltpu.SMEM(tile_coord.shape, jnp.int32),
                pltpu.SMEM(tile_count.shape, jnp.int32),
                pltpu.VMEM((n_src, n_tgt * tile, tile) if small else (1, 16, 128), BF16),
                pltpu.VMEM((halves, n_tgt * tile, half), F32),
                pltpu.VMEM((halves, n_row - 1, rows, half), BF16),
                pltpu.VMEM((halves, n_row - 1, rows, half), BF16),
                dma((2,)), dma((halves,)), dma, dma,
                dma((halves, n_z)), dma((halves, n_z)),
                dma((halves, n_y, n_z)), dma((halves, n_y, n_z)),
                dma((halves, n_row - 1)), dma((halves, n_row - 1)),
            ],
            compiler_params=pltpu.CompilerParams(
                collective_id=0, has_side_effects=True, vmem_limit_bytes=64 * 2**20
            ),
        )(features, adj_tiles, tile_coord, tile_count, weight)

    return jax.shard_map(
        on_device,
        mesh=mesh,
        in_specs=(
            P(("row", "col"), None),
            P("row", "col", None, None, None),
            P("row", "col", None),
            P("row", "col"),
            P(),
        ),
        out_specs=P(("col", "row"), None),
        check_vma=False,
    )
```

```python
import functools

import jax
import jax.numpy as jnp
from jax import lax
from jax.experimental import pallas as pl
from jax.experimental.pallas import tpu as pltpu
from jax.sharding import PartitionSpec as P

MESH = pl.DeviceIdType.MESH
F32 = jnp.float32
BF16 = jnp.bfloat16


def kernel(
    n_row, n_z, n_y,
    x_ref, adj_ref, coord_ref, count_ref, w_ref, out_ref,
    feats, adj, weight, coord, count, dense, total, stage, parts,
    int_sems, own_sems, adj_sem, weight_sem, z_send, z_recv, y_send, y_recv, row_send, row_recv,
):
    row, col = lax.axis_index("row"), lax.axis_index("col")
    z, y = col // n_y, col % n_y
    slots, tile = adj_ref.shape[2], adj_ref.shape[3]
    rows = x_ref.shape[0]
    halves, _, width = feats.shape
    n_tgt = n_row * rows // tile
    n_src = n_z * n_y * rows // tile
    row_order = sorted(range(1, n_row), key=lambda d: d % 2)

    def piece(h, z_at, y_at):
        return feats.at[h, pl.ds(pl.multiple_of((z_at * n_y + y_at) * rows, rows), rows)]

    def z_peer(d):
        return {"col": lax.rem(z + d, n_z) * n_y + y}

    def y_peer(e):
        return {"col": z * n_y + lax.rem(y + e, n_y)}

    def row_peer(d):
        return {"row": lax.rem(row + d, n_row)}

    def back(at, d, n):
        return lax.rem(at + n - d, n)

    own_copies = [
        pltpu.make_async_copy(x_ref.at[:, pl.ds(h * width, width)], piece(h, z, y), own_sems.at[h])
        for h in range(halves)
    ]
    for copy in own_copies:
        copy.start()
    coord_copy = pltpu.make_async_copy(coord_ref, coord, int_sems.at[0])
    coord_copy.start()
    count_copy = pltpu.make_async_copy(count_ref, count, int_sems.at[1])
    count_copy.start()
    adj_copy = pltpu.make_async_copy(adj_ref.at[0, 0], adj, adj_sem)
    adj_copy.start()
    weight_copy = pltpu.make_async_copy(w_ref, weight, weight_sem)
    weight_copy.start()

    barrier = pltpu.get_barrier_semaphore()
    peers = [z_peer(d) for d in range(1, n_z)]
    peers += [y_peer(e) for e in range(1, n_y)]
    peers += [row_peer(d) for d in range(1, n_row)]
    for peer in peers:
        pl.semaphore_signal(barrier, inc=1, device_id=peer, device_id_type=MESH)
    pl.semaphore_wait(barrier, len(peers))

    def z_copy(h, d, block):
        return pltpu.make_async_remote_copy(
            src_ref=block, dst_ref=block, send_sem=z_send.at[h, d], recv_sem=z_recv.at[h, d],
            device_id=z_peer(d), device_id_type=MESH,
        )

    def y_copy(h, e, d, block):
        return pltpu.make_async_remote_copy(
            src_ref=block, dst_ref=block, send_sem=y_send.at[h, e, d], recv_sem=y_recv.at[h, e, d],
            device_id=y_peer(e), device_id_type=MESH,
        )

    for h in range(halves):
        own_copies[h].wait()
        for d in range(1, n_z):
            z_copy(h, d, piece(h, z, y)).start()
        for e in range(1, n_y):
            y_copy(h, e, 0, piece(h, z, y)).start()

    coord_copy.wait()
    count_copy.wait()
    adj_copy.wait()
    small = slots <= 8 and n_y * rows == tile

    def live(k):
        return jnp.where(k < count[0, 0], coord[0, 0, k], -1)

    if small:
        for s in range(n_src):
            for t in range(n_tgt):
                block = jnp.zeros((tile, tile), F32)
                for k in range(slots):
                    keep = jnp.where(live(k) == t * n_src + s, 1.0, 0.0).astype(F32)
                    block = block + adj[k].astype(F32) * keep
                dense[s, pl.ds(t * tile, tile), :] = block.astype(BF16)

    for h in range(halves):
        for d in range(1, n_z):
            block = piece(h, back(z, d, n_z), y)
            z_copy(h, d, block).wait_recv()
            for e in range(1, n_y):
                y_copy(h, e, d, block).start()

    def row_copy(h, d):
        return pltpu.make_async_remote_copy(
            src_ref=stage.at[h, d - 1], dst_ref=parts.at[h, d - 1],
            send_sem=row_send.at[h, d - 1], recv_sem=row_recv.at[h, d - 1],
            device_id=row_peer(d), device_id_type=MESH,
        )

    def block_of(h, r):
        return total[h, pl.ds(pl.multiple_of(r * rows, rows), rows), :]

    for h in range(halves):
        product = None
        for d in range(n_z):
            z_from = back(z, d, n_z)
            for e in range(1, n_y):
                y_copy(h, e, d, piece(h, z_from, back(y, e, n_y))).wait_recv()
            if small:
                values = feats[h, pl.ds(pl.multiple_of(z_from * tile, tile), tile), :]
                term = jnp.dot(dense[z_from], values, preferred_element_type=F32)
                product = term if d == 0 else product + term
        if small:
            total[h] = product
        else:
            total[h] = jnp.zeros(total.shape[1:], F32)

            def add_slot(k, carry):
                at = live(k)
                source = jnp.where(at < 0, 0, lax.rem(at, n_src))
                values = feats[h, pl.ds(pl.multiple_of(source * tile, tile), tile), :]
                term = jnp.dot(adj[k], values, preferred_element_type=F32)
                for t in range(n_tgt):
                    own = jnp.logical_and(at >= t * n_src, at < (t + 1) * n_src)
                    total[h, pl.ds(t * tile, tile), :] += term * jnp.where(own, 1.0, 0.0).astype(F32)
                return carry

            lax.fori_loop(0, slots, add_slot, 0)
        for d in row_order:
            stage[h, d - 1] = block_of(h, lax.rem(row + d, n_row)).astype(stage.dtype)
            row_copy(h, d).start()

    weight_copy.wait()
    mixed = None
    for h in range(halves):
        hidden = block_of(h, row)
        for d in reversed(row_order):
            row_copy(h, d).wait_recv()
            hidden = hidden + parts[h, d - 1].astype(F32)
        term = jnp.dot(
            hidden.astype(BF16), weight[pl.ds(h * width, width), :], preferred_element_type=F32
        )
        mixed = term if h == 0 else mixed + term
    out_ref[...] = jnp.maximum(mixed, 0.0).astype(out_ref.dtype)

    for h in range(halves):
        for d in range(1, n_z):
            z_copy(h, d, piece(h, z, y)).wait_send()
        for d in range(n_z):
            for e in range(1, n_y):
                y_copy(h, e, d, piece(h, back(z, d, n_z), y)).wait_send()
        for d in range(1, n_row):
            row_copy(h, d).wait_send()


def pair_kernel(
    n_row, n_col,
    x_ref, adj_ref, coord_ref, count_ref, w_ref, out_ref,
    own, feats, adj, weight, coord, code, dense, total, stage, parts,
    coord_sem, own_sems, adj_sem, weight_sem,
    pair_send, pair_recv, col_send, col_recv, row_send, row_recv,
):
    row, col = lax.axis_index("row"), lax.axis_index("col")
    side = col % 2
    pair = col + 1 - 2 * side
    slots, tile = adj_ref.shape[2], adj_ref.shape[3]
    rows, half = x_ref.shape[0], feats.shape[1]
    n_tgt, n_src = n_row * rows // tile, n_col * rows // tile
    targets = n_tgt * tile

    def piece(c):
        return feats.at[pl.ds(pl.multiple_of(c * rows, rows), rows)]

    def columns(h):
        return x_ref.at[:, pl.ds(pl.multiple_of(h * half, half), half)]

    coord_copy = pltpu.make_async_copy(coord_ref, coord, coord_sem)
    adj_copy = pltpu.make_async_copy(adj_ref.at[0, 0], adj.at[0], adj_sem)
    weight_copy = pltpu.make_async_copy(w_ref, weight, weight_sem)
    own_copies = [pltpu.make_async_copy(columns(h), own.at[h], own_sems.at[h]) for h in range(2)]
    own_copies.append(pltpu.make_async_copy(columns(side), piece(col), own_sems.at[2]))
    row_peers = [(e, d) for d in range(n_row) for e in range(2) if e + d > 0]
    row_peers.sort(key=lambda ed: (ed[1] % 2, -ed[1]))

    def row_peer(e, d):
        return {"row": lax.rem(row + d, n_row), "col": pair if e else col}

    barrier = pltpu.get_barrier_semaphore()
    peers = [{"col": lax.rem(col + d, n_col)} for d in range(1, n_col)]
    peers += [row_peer(e, d) for e, d in row_peers if d > 0]
    for peer in peers:
        pl.semaphore_signal(barrier, inc=1, device_id=peer, device_id_type=MESH)
    for copy in own_copies + [coord_copy, adj_copy, weight_copy]:
        copy.start()
    pl.semaphore_wait(barrier, len(peers))

    pair_adj = pltpu.make_async_remote_copy(
        src_ref=adj_ref.at[0, 0], dst_ref=adj.at[1], send_sem=pair_send.at[0],
        recv_sem=pair_recv.at[0], device_id={"col": pair}, device_id_type=MESH,
    )
    pair_adj.start()
    for copy in own_copies:
        copy.wait()

    def col_copy(d):
        return pltpu.make_async_remote_copy(
            src_ref=own.at[lax.rem(side + d, 2)], dst_ref=piece(col), send_sem=col_send.at[d],
            recv_sem=col_recv.at[col], device_id={"col": lax.rem(col + d, n_col)},
            device_id_type=MESH,
        )

    for d in range(1, n_col):
        col_copy(d).start()

    coord_copy.wait()
    for k in range(slots):
        at = jnp.where(k < count_ref[0, 0], coord[0, 0, k], -1)
        code[0, pl.ds(k, 1), :] = jnp.full((1, tile), at, jnp.int32)
    pair_code = pltpu.make_async_remote_copy(
        src_ref=code.at[0], dst_ref=code.at[1], send_sem=pair_send.at[1],
        recv_sem=pair_recv.at[1], device_id={"col": pair}, device_id_type=MESH,
    )
    pair_code.start()

    def spread(e):
        for s in range(n_src):
            for t in range(n_tgt):
                block = jnp.zeros((tile, tile), F32)
                for k in range(slots):
                    keep = jnp.where(code[e, pl.ds(k, 1), :] == t * n_src + s, 1.0, 0.0).astype(F32)
                    block = block + adj[e, k].astype(F32) * keep
                dense[s, pl.ds(e * targets + t * tile, tile), :] = block.astype(BF16)

    adj_copy.wait()
    spread(0)
    pair_adj.wait_recv()
    pair_code.wait_recv()
    spread(1)

    def arrived(c):
        pltpu.make_async_remote_copy(
            src_ref=own.at[0], dst_ref=piece(c), send_sem=col_send.at[0],
            recv_sem=col_recv.at[c], device_id={"col": pair}, device_id_type=MESH,
        ).wait_recv()

    product = None
    for q in range(n_src):
        s = lax.rem(col // 2 + q, n_src)
        if q == 0:
            arrived(pair)
        else:
            arrived(2 * s)
            arrived(2 * s + 1)
        values = feats[pl.ds(pl.multiple_of(s * tile, tile), tile), :]
        term = jnp.dot(dense[s], values, preferred_element_type=F32)
        product = term if q == 0 else product + term
    total[...] = product

    def row_copy(e, d):
        return pltpu.make_async_remote_copy(
            src_ref=stage.at[e, d], dst_ref=parts.at[e, d], send_sem=row_send.at[e, d],
            recv_sem=row_recv.at[e, d], device_id=row_peer(e, d), device_id_type=MESH,
        )

    def block_of(e, r):
        return total[pl.ds(pl.multiple_of(e * targets + r * rows, rows), rows), :]

    for e, d in row_peers:
        stage[e, d] = block_of(e, lax.rem(row + d, n_row)).astype(stage.dtype)
        row_copy(e, d).start()
    weight_copy.wait()
    hidden = [block_of(0, row), jnp.zeros((rows, half), F32)]
    for e, d in reversed(row_peers):
        row_copy(e, d).wait_recv()
        hidden[e] = hidden[e] + parts[e, d].astype(F32)

    def weight_rows(h):
        return weight[pl.ds(pl.multiple_of(h * half, half), half), :]

    mixed = jnp.dot(hidden[0].astype(BF16), weight_rows(side), preferred_element_type=F32)
    mixed += jnp.dot(hidden[1].astype(BF16), weight_rows(1 - side), preferred_element_type=F32)
    out_ref[...] = jnp.maximum(mixed, 0.0).astype(out_ref.dtype)

    pair_adj.wait_send()
    pair_code.wait_send()
    for d in range(1, n_col):
        col_copy(d).wait_send()
    for e, d in row_peers:
        row_copy(e, d).wait_send()


def hbm(array):
    return pltpu.with_memory_space_constraint(array, pltpu.HBM)


def pair_call(n_row, n_col, features, adj_tiles, tile_coord, tile_count, weight):
    rows, width = features.shape
    slots, tile = adj_tiles.shape[2:4]
    targets, n_src, half = n_row * rows, n_col * rows // tile, width // 2
    dma = pltpu.SemaphoreType.DMA
    in_hbm = pl.BlockSpec(memory_space=pltpu.HBM)
    return pl.pallas_call(
        functools.partial(pair_kernel, n_row, n_col),
        out_shape=jax.ShapeDtypeStruct((rows, weight.shape[1]), BF16),
        in_specs=[in_hbm, in_hbm, in_hbm, pl.BlockSpec(memory_space=pltpu.SMEM), in_hbm],
        out_specs=pl.BlockSpec(memory_space=pltpu.VMEM),
        scratch_shapes=[
            pltpu.VMEM((2, rows, half), BF16),
            pltpu.VMEM((n_col * rows, half), BF16),
            pltpu.VMEM((2, slots, tile, tile), BF16),
            pltpu.VMEM(weight.shape, BF16),
            pltpu.SMEM(tile_coord.shape, jnp.int32),
            pltpu.VMEM((2, 8, tile), jnp.int32),
            pltpu.VMEM((n_src, 2 * targets, tile), BF16),
            pltpu.VMEM((2 * targets, half), F32),
            pltpu.VMEM((2, n_row, rows, half), BF16),
            pltpu.VMEM((2, n_row, rows, half), BF16),
            dma, dma((3,)), dma, dma,
            dma((2,)), dma((2,)),
            dma((n_col,)), dma((n_col,)),
            dma((2, n_row)), dma((2, n_row)),
        ],
        compiler_params=pltpu.CompilerParams(
            collective_id=0, has_side_effects=True, vmem_limit_bytes=32 * 2**20
        ),
    )(hbm(features), hbm(adj_tiles), hbm(tile_coord), tile_count, hbm(weight))


def solution(mesh):
    n_row, n_col = mesh.shape["row"], mesh.shape["col"]
    n_y = max(1, n_row // 2)
    if n_col % n_y:
        n_y = 1
    n_z = n_col // n_y

    def on_device(features, adj_tiles, tile_coord, tile_count, weight):
        rows, width = features.shape
        slots, tile = adj_tiles.shape[2:4]
        n_tgt = n_row * rows // tile
        n_src = n_col * rows // tile
        paired = slots <= 8 and 2 * rows == tile and width == 2 * tile and n_col % 2 == 0
        if paired:
            return pair_call(n_row, n_col, features, adj_tiles, tile_coord, tile_count, weight)
        small = slots <= 8 and n_y * rows == tile
        in_hbm = pl.BlockSpec(memory_space=pltpu.HBM)
        dma = pltpu.SemaphoreType.DMA
        halves = 2
        half = width // halves
        return pl.pallas_call(
            functools.partial(kernel, n_row, n_z, n_y),
            out_shape=jax.ShapeDtypeStruct((rows, weight.shape[1]), BF16),
            in_specs=[in_hbm] * 5,
            out_specs=pl.BlockSpec(memory_space=pltpu.VMEM),
            scratch_shapes=[
                pltpu.VMEM((halves, n_col * rows, half), BF16),
                pltpu.VMEM((slots, tile, tile), BF16),
                pltpu.VMEM(weight.shape, BF16),
                pltpu.SMEM(tile_coord.shape, jnp.int32),
                pltpu.SMEM(tile_count.shape, jnp.int32),
                pltpu.VMEM((n_src, n_tgt * tile, tile) if small else (1, 16, 128), BF16),
                pltpu.VMEM((halves, n_tgt * tile, half), F32),
                pltpu.VMEM((halves, n_row - 1, rows, half), BF16),
                pltpu.VMEM((halves, n_row - 1, rows, half), BF16),
                dma((2,)), dma((halves,)), dma, dma,
                dma((halves, n_z)), dma((halves, n_z)),
                dma((halves, n_y, n_z)), dma((halves, n_y, n_z)),
                dma((halves, n_row - 1)), dma((halves, n_row - 1)),
            ],
            compiler_params=pltpu.CompilerParams(
                collective_id=0, has_side_effects=True, vmem_limit_bytes=32 * 2**20
            ),
        )(hbm(features), hbm(adj_tiles), hbm(tile_coord), tile_count, hbm(weight))

    return jax.shard_map(
        on_device,
        mesh=mesh,
        in_specs=(
            P(("row", "col"), None),
            P("row", "col", None, None, None),
            P("row", "col", None),
            P("row", "col"),
            P(),
        ),
        out_specs=P(("col", "row"), None),
        check_vma=False,
    )
```

```python
import functools

import jax
import jax.numpy as jnp
from jax import lax
from jax.experimental import pallas as pl
from jax.experimental.pallas import tpu as pltpu
from jax.sharding import PartitionSpec as P

MESH = pl.DeviceIdType.MESH
F32 = jnp.float32
BF16 = jnp.bfloat16


def kernel(
    n_row, n_z, n_y,
    x_ref, adj_ref, coord_ref, count_ref, w_ref, out_ref,
    feats, adj, weight, coord, count, dense, total, stage, parts,
    int_sems, own_sems, adj_sem, weight_sem, z_send, z_recv, y_send, y_recv, row_send, row_recv,
):
    row, col = lax.axis_index("row"), lax.axis_index("col")
    z, y = col // n_y, col % n_y
    slots, tile = adj_ref.shape[2], adj_ref.shape[3]
    rows = x_ref.shape[0]
    halves, _, width = feats.shape
    n_tgt = n_row * rows // tile
    n_src = n_z * n_y * rows // tile
    row_order = sorted(range(1, n_row), key=lambda d: d % 2)

    def piece(h, z_at, y_at):
        return feats.at[h, pl.ds(pl.multiple_of((z_at * n_y + y_at) * rows, rows), rows)]

    def z_peer(d):
        return {"col": lax.rem(z + d, n_z) * n_y + y}

    def y_peer(e):
        return {"col": z * n_y + lax.rem(y + e, n_y)}

    def row_peer(d):
        return {"row": lax.rem(row + d, n_row)}

    def back(at, d, n):
        return lax.rem(at + n - d, n)

    own_copies = [
        pltpu.make_async_copy(x_ref.at[:, pl.ds(h * width, width)], piece(h, z, y), own_sems.at[h])
        for h in range(halves)
    ]
    for copy in own_copies:
        copy.start()
    coord_copy = pltpu.make_async_copy(coord_ref, coord, int_sems.at[0])
    coord_copy.start()
    count_copy = pltpu.make_async_copy(count_ref, count, int_sems.at[1])
    count_copy.start()
    adj_copy = pltpu.make_async_copy(adj_ref.at[0, 0], adj, adj_sem)
    adj_copy.start()
    weight_copy = pltpu.make_async_copy(w_ref, weight, weight_sem)
    weight_copy.start()

    barrier = pltpu.get_barrier_semaphore()
    peers = [z_peer(d) for d in range(1, n_z)]
    peers += [y_peer(e) for e in range(1, n_y)]
    peers += [row_peer(d) for d in range(1, n_row)]
    for peer in peers:
        pl.semaphore_signal(barrier, inc=1, device_id=peer, device_id_type=MESH)
    pl.semaphore_wait(barrier, len(peers))

    def z_copy(h, d, block):
        return pltpu.make_async_remote_copy(
            src_ref=block, dst_ref=block, send_sem=z_send.at[h, d], recv_sem=z_recv.at[h, d],
            device_id=z_peer(d), device_id_type=MESH,
        )

    def y_copy(h, e, d, block):
        return pltpu.make_async_remote_copy(
            src_ref=block, dst_ref=block, send_sem=y_send.at[h, e, d], recv_sem=y_recv.at[h, e, d],
            device_id=y_peer(e), device_id_type=MESH,
        )

    for h in range(halves):
        own_copies[h].wait()
        for d in range(1, n_z):
            z_copy(h, d, piece(h, z, y)).start()
        for e in range(1, n_y):
            y_copy(h, e, 0, piece(h, z, y)).start()

    coord_copy.wait()
    count_copy.wait()
    adj_copy.wait()
    small = slots <= 8 and n_y * rows == tile

    def live(k):
        return jnp.where(k < count[0, 0], coord[0, 0, k], -1)

    if small:
        for s in range(n_src):
            for t in range(n_tgt):
                block = jnp.zeros((tile, tile), F32)
                for k in range(slots):
                    keep = jnp.where(live(k) == t * n_src + s, 1.0, 0.0).astype(F32)
                    block = block + adj[k].astype(F32) * keep
                dense[s, pl.ds(t * tile, tile), :] = block.astype(BF16)

    for h in range(halves):
        for d in range(1, n_z):
            block = piece(h, back(z, d, n_z), y)
            z_copy(h, d, block).wait_recv()
            for e in range(1, n_y):
                y_copy(h, e, d, block).start()

    def row_copy(h, d):
        return pltpu.make_async_remote_copy(
            src_ref=stage.at[h, d - 1], dst_ref=parts.at[h, d - 1],
            send_sem=row_send.at[h, d - 1], recv_sem=row_recv.at[h, d - 1],
            device_id=row_peer(d), device_id_type=MESH,
        )

    def block_of(h, r):
        return total[h, pl.ds(pl.multiple_of(r * rows, rows), rows), :]

    for h in range(halves):
        product = None
        for d in range(n_z):
            z_from = back(z, d, n_z)
            for e in range(1, n_y):
                y_copy(h, e, d, piece(h, z_from, back(y, e, n_y))).wait_recv()
            if small:
                values = feats[h, pl.ds(pl.multiple_of(z_from * tile, tile), tile), :]
                term = jnp.dot(dense[z_from], values, preferred_element_type=F32)
                product = term if d == 0 else product + term
        if small:
            total[h] = product
        else:
            total[h] = jnp.zeros(total.shape[1:], F32)

            def add_slot(k, carry):
                at = live(k)
                source = jnp.where(at < 0, 0, lax.rem(at, n_src))
                values = feats[h, pl.ds(pl.multiple_of(source * tile, tile), tile), :]
                term = jnp.dot(adj[k], values, preferred_element_type=F32)
                for t in range(n_tgt):
                    own = jnp.logical_and(at >= t * n_src, at < (t + 1) * n_src)
                    total[h, pl.ds(t * tile, tile), :] += term * jnp.where(own, 1.0, 0.0).astype(F32)
                return carry

            lax.fori_loop(0, slots, add_slot, 0)
        for d in row_order:
            stage[h, d - 1] = block_of(h, lax.rem(row + d, n_row)).astype(stage.dtype)
            row_copy(h, d).start()

    weight_copy.wait()
    mixed = None
    for h in range(halves):
        hidden = block_of(h, row)
        for d in reversed(row_order):
            row_copy(h, d).wait_recv()
            hidden = hidden + parts[h, d - 1].astype(F32)
        term = jnp.dot(
            hidden.astype(BF16), weight[pl.ds(h * width, width), :], preferred_element_type=F32
        )
        mixed = term if h == 0 else mixed + term
    out_ref[...] = jnp.maximum(mixed, 0.0).astype(out_ref.dtype)

    for h in range(halves):
        for d in range(1, n_z):
            z_copy(h, d, piece(h, z, y)).wait_send()
        for d in range(n_z):
            for e in range(1, n_y):
                y_copy(h, e, d, piece(h, back(z, d, n_z), y)).wait_send()
        for d in range(1, n_row):
            row_copy(h, d).wait_send()


def pair_kernel(
    n_row, n_col,
    x_ref, adj_ref, coord_ref, count_ref, w_ref, out_ref,
    feats, adj, weight, coord, code, dense, total, stage, parts,
    coord_sem, own_sem, adj_sem, weight_sem,
    pair_send, pair_recv, col_send, col_recv, row_send, row_recv,
):
    row, col = lax.axis_index("row"), lax.axis_index("col")
    side = col % 2
    pair = col + 1 - 2 * side
    slots, tile = adj_ref.shape[2], adj_ref.shape[3]
    rows, half = x_ref.shape[0], feats.shape[1]
    n_tgt, n_src = n_row * rows // tile, n_col * rows // tile
    targets = n_tgt * tile

    def piece(c):
        return feats.at[pl.ds(pl.multiple_of(c * rows, rows), rows)]

    def columns(h):
        return x_ref.at[:, pl.ds(pl.multiple_of(h * half, half), half)]

    coord_copy = pltpu.make_async_copy(coord_ref, coord, coord_sem)
    adj_copy = pltpu.make_async_copy(adj_ref.at[0, 0], adj.at[0], adj_sem)
    weight_copy = pltpu.make_async_copy(w_ref, weight, weight_sem)
    own_copy = pltpu.make_async_copy(columns(side), piece(col), own_sem)
    row_peers = [(e, d) for d in range(n_row) for e in range(2) if e + d > 0]
    row_peers.sort(key=lambda ed: (ed[1] % 2, -ed[1]))

    def row_peer(e, d):
        return {"row": lax.rem(row + d, n_row), "col": pair if e else col}

    barrier = pltpu.get_barrier_semaphore()
    peers = [{"col": lax.rem(col + d, n_col)} for d in range(1, n_col)]
    peers += [row_peer(e, d) for e, d in row_peers if d > 0]
    for peer in peers:
        pl.semaphore_signal(barrier, inc=1, device_id=peer, device_id_type=MESH)
    for copy in (coord_copy, adj_copy, own_copy, weight_copy):
        copy.start()
    pl.semaphore_wait(barrier, len(peers))

    pair_adj = pltpu.make_async_remote_copy(
        src_ref=adj_ref.at[0, 0], dst_ref=adj.at[1], send_sem=pair_send.at[0],
        recv_sem=pair_recv.at[0], device_id={"col": pair}, device_id_type=MESH,
    )

    def col_copy(d):
        return pltpu.make_async_remote_copy(
            src_ref=columns(lax.rem(side + d, 2)), dst_ref=piece(col), send_sem=col_send.at[d],
            recv_sem=col_recv.at[col], device_id={"col": lax.rem(col + d, n_col)},
            device_id_type=MESH,
        )

    for d in range(1, n_col):
        col_copy(d).start()
    pair_adj.start()

    coord_copy.wait()
    for k in range(slots):
        at = jnp.where(k < count_ref[0, 0], coord[0, 0, k], -1)
        code[0, pl.ds(k, 1), :] = jnp.full((1, tile), at, jnp.int32)
    pair_code = pltpu.make_async_remote_copy(
        src_ref=code.at[0], dst_ref=code.at[1], send_sem=pair_send.at[1],
        recv_sem=pair_recv.at[1], device_id={"col": pair}, device_id_type=MESH,
    )
    pair_code.start()

    def spread(e):
        for s in range(n_src):
            for t in range(n_tgt):
                block = jnp.zeros((tile, tile), F32)
                for k in range(slots):
                    keep = jnp.where(code[e, pl.ds(k, 1), :] == t * n_src + s, 1.0, 0.0).astype(F32)
                    block = block + adj[e, k].astype(F32) * keep
                dense[s, pl.ds(e * targets + t * tile, tile), :] = block.astype(BF16)

    adj_copy.wait()
    spread(0)
    pair_adj.wait_recv()
    pair_code.wait_recv()
    spread(1)

    def arrived(c):
        pltpu.make_async_remote_copy(
            src_ref=columns(0), dst_ref=piece(c), send_sem=col_send.at[0],
            recv_sem=col_recv.at[c], device_id={"col": pair}, device_id_type=MESH,
        ).wait_recv()

    own_copy.wait()
    product = None
    for q in range(n_src):
        s = lax.rem(col // 2 + q, n_src)
        if q == 0:
            arrived(pair)
        else:
            arrived(2 * s)
            arrived(2 * s + 1)
        values = feats[pl.ds(pl.multiple_of(s * tile, tile), tile), :]
        term = jnp.dot(dense[s], values, preferred_element_type=F32)
        product = term if q == 0 else product + term
    total[...] = product

    def row_copy(e, d):
        return pltpu.make_async_remote_copy(
            src_ref=stage.at[e, d], dst_ref=parts.at[e, d], send_sem=row_send.at[e, d],
            recv_sem=row_recv.at[e, d], device_id=row_peer(e, d), device_id_type=MESH,
        )

    def block_of(e, r):
        return total[pl.ds(pl.multiple_of(e * targets + r * rows, rows), rows), :]

    for e, d in row_peers:
        stage[e, d] = block_of(e, lax.rem(row + d, n_row)).astype(stage.dtype)
        row_copy(e, d).start()
    weight_copy.wait()
    hidden = [block_of(0, row), jnp.zeros((rows, half), F32)]
    for e, d in reversed(row_peers):
        row_copy(e, d).wait_recv()
        hidden[e] = hidden[e] + parts[e, d].astype(F32)

    def weight_rows(h):
        return weight[pl.ds(pl.multiple_of(h * half, half), half), :]

    mixed = jnp.dot(hidden[0].astype(BF16), weight_rows(side), preferred_element_type=F32)
    mixed += jnp.dot(hidden[1].astype(BF16), weight_rows(1 - side), preferred_element_type=F32)
    out_ref[...] = jnp.maximum(mixed, 0.0).astype(out_ref.dtype)

    pair_adj.wait_send()
    pair_code.wait_send()
    for d in range(1, n_col):
        col_copy(d).wait_send()
    for e, d in row_peers:
        row_copy(e, d).wait_send()


def hbm(array):
    return pltpu.with_memory_space_constraint(array, pltpu.HBM)


def pair_call(n_row, n_col, features, adj_tiles, tile_coord, tile_count, weight):
    rows, width = features.shape
    slots, tile = adj_tiles.shape[2:4]
    targets, n_src, half = n_row * rows, n_col * rows // tile, width // 2
    dma = pltpu.SemaphoreType.DMA
    in_hbm = pl.BlockSpec(memory_space=pltpu.HBM)
    return pl.pallas_call(
        functools.partial(pair_kernel, n_row, n_col),
        out_shape=jax.ShapeDtypeStruct((rows, weight.shape[1]), BF16),
        in_specs=[in_hbm, in_hbm, in_hbm, pl.BlockSpec(memory_space=pltpu.SMEM), in_hbm],
        out_specs=pl.BlockSpec(memory_space=pltpu.VMEM),
        scratch_shapes=[
            pltpu.VMEM((n_col * rows, half), BF16),
            pltpu.VMEM((2, slots, tile, tile), BF16),
            pltpu.VMEM(weight.shape, BF16),
            pltpu.SMEM(tile_coord.shape, jnp.int32),
            pltpu.VMEM((2, 8, tile), jnp.int32),
            pltpu.VMEM((n_src, 2 * targets, tile), BF16),
            pltpu.VMEM((2 * targets, half), F32),
            pltpu.VMEM((2, n_row, rows, half), BF16),
            pltpu.VMEM((2, n_row, rows, half), BF16),
            dma, dma, dma, dma,
            dma((2,)), dma((2,)),
            dma((n_col,)), dma((n_col,)),
            dma((2, n_row)), dma((2, n_row)),
        ],
        compiler_params=pltpu.CompilerParams(
            collective_id=0, has_side_effects=True, vmem_limit_bytes=32 * 2**20
        ),
    )(hbm(features), hbm(adj_tiles), hbm(tile_coord), tile_count, hbm(weight))


def solution(mesh):
    n_row, n_col = mesh.shape["row"], mesh.shape["col"]
    n_y = max(1, n_row // 2)
    if n_col % n_y:
        n_y = 1
    n_z = n_col // n_y

    def on_device(features, adj_tiles, tile_coord, tile_count, weight):
        rows, width = features.shape
        slots, tile = adj_tiles.shape[2:4]
        n_tgt = n_row * rows // tile
        n_src = n_col * rows // tile
        paired = slots <= 8 and 2 * rows == tile and width == 2 * tile and n_col % 2 == 0
        if paired:
            return pair_call(n_row, n_col, features, adj_tiles, tile_coord, tile_count, weight)
        small = slots <= 8 and n_y * rows == tile
        in_hbm = pl.BlockSpec(memory_space=pltpu.HBM)
        dma = pltpu.SemaphoreType.DMA
        halves = 2
        half = width // halves
        return pl.pallas_call(
            functools.partial(kernel, n_row, n_z, n_y),
            out_shape=jax.ShapeDtypeStruct((rows, weight.shape[1]), BF16),
            in_specs=[in_hbm] * 5,
            out_specs=pl.BlockSpec(memory_space=pltpu.VMEM),
            scratch_shapes=[
                pltpu.VMEM((halves, n_col * rows, half), BF16),
                pltpu.VMEM((slots, tile, tile), BF16),
                pltpu.VMEM(weight.shape, BF16),
                pltpu.SMEM(tile_coord.shape, jnp.int32),
                pltpu.SMEM(tile_count.shape, jnp.int32),
                pltpu.VMEM((n_src, n_tgt * tile, tile) if small else (1, 16, 128), BF16),
                pltpu.VMEM((halves, n_tgt * tile, half), F32),
                pltpu.VMEM((halves, n_row - 1, rows, half), BF16),
                pltpu.VMEM((halves, n_row - 1, rows, half), BF16),
                dma((2,)), dma((halves,)), dma, dma,
                dma((halves, n_z)), dma((halves, n_z)),
                dma((halves, n_y, n_z)), dma((halves, n_y, n_z)),
                dma((halves, n_row - 1)), dma((halves, n_row - 1)),
            ],
            compiler_params=pltpu.CompilerParams(
                collective_id=0, has_side_effects=True, vmem_limit_bytes=32 * 2**20
            ),
        )(hbm(features), hbm(adj_tiles), hbm(tile_coord), tile_count, hbm(weight))

    return jax.shard_map(
        on_device,
        mesh=mesh,
        in_specs=(
            P(("row", "col"), None),
            P("row", "col", None, None, None),
            P("row", "col", None),
            P("row", "col"),
            P(),
        ),
        out_specs=P(("col", "row"), None),
        check_vma=False,
    )
```

```python
import functools

import jax
import jax.numpy as jnp
from jax import lax
from jax.experimental import pallas as pl
from jax.experimental.pallas import tpu as pltpu
from jax.sharding import PartitionSpec as P

MESH = pl.DeviceIdType.MESH
F32 = jnp.float32
BF16 = jnp.bfloat16


def kernel(
    n_row, n_z, n_y,
    x_ref, adj_ref, coord_ref, count_ref, w_ref, out_ref,
    feats, adj, weight, coord, count, dense, total, stage, parts,
    int_sems, own_sems, adj_sem, weight_sem, z_send, z_recv, y_send, y_recv, row_send, row_recv,
):
    row, col = lax.axis_index("row"), lax.axis_index("col")
    z, y = col // n_y, col % n_y
    slots, tile = adj_ref.shape[2], adj_ref.shape[3]
    rows = x_ref.shape[0]
    halves, _, width = feats.shape
    n_tgt = n_row * rows // tile
    n_src = n_z * n_y * rows // tile
    row_order = sorted(range(1, n_row), key=lambda d: d % 2)

    def piece(h, z_at, y_at):
        return feats.at[h, pl.ds(pl.multiple_of((z_at * n_y + y_at) * rows, rows), rows)]

    def z_peer(d):
        return {"col": lax.rem(z + d, n_z) * n_y + y}

    def y_peer(e):
        return {"col": z * n_y + lax.rem(y + e, n_y)}

    def row_peer(d):
        return {"row": lax.rem(row + d, n_row)}

    def back(at, d, n):
        return lax.rem(at + n - d, n)

    own_copies = [
        pltpu.make_async_copy(x_ref.at[:, pl.ds(h * width, width)], piece(h, z, y), own_sems.at[h])
        for h in range(halves)
    ]
    for copy in own_copies:
        copy.start()
    coord_copy = pltpu.make_async_copy(coord_ref, coord, int_sems.at[0])
    coord_copy.start()
    count_copy = pltpu.make_async_copy(count_ref, count, int_sems.at[1])
    count_copy.start()
    adj_copy = pltpu.make_async_copy(adj_ref.at[0, 0], adj, adj_sem)
    adj_copy.start()
    weight_copy = pltpu.make_async_copy(w_ref, weight, weight_sem)
    weight_copy.start()

    barrier = pltpu.get_barrier_semaphore()
    peers = [z_peer(d) for d in range(1, n_z)]
    peers += [y_peer(e) for e in range(1, n_y)]
    peers += [row_peer(d) for d in range(1, n_row)]
    for peer in peers:
        pl.semaphore_signal(barrier, inc=1, device_id=peer, device_id_type=MESH)
    pl.semaphore_wait(barrier, len(peers))

    def z_copy(h, d, block):
        return pltpu.make_async_remote_copy(
            src_ref=block, dst_ref=block, send_sem=z_send.at[h, d], recv_sem=z_recv.at[h, d],
            device_id=z_peer(d), device_id_type=MESH,
        )

    def y_copy(h, e, d, block):
        return pltpu.make_async_remote_copy(
            src_ref=block, dst_ref=block, send_sem=y_send.at[h, e, d], recv_sem=y_recv.at[h, e, d],
            device_id=y_peer(e), device_id_type=MESH,
        )

    for h in range(halves):
        own_copies[h].wait()
        for d in range(1, n_z):
            z_copy(h, d, piece(h, z, y)).start()
        for e in range(1, n_y):
            y_copy(h, e, 0, piece(h, z, y)).start()

    coord_copy.wait()
    count_copy.wait()
    adj_copy.wait()
    small = slots <= 8 and n_y * rows == tile

    def live(k):
        return jnp.where(k < count[0, 0], coord[0, 0, k], -1)

    if small:
        for s in range(n_src):
            for t in range(n_tgt):
                block = jnp.zeros((tile, tile), F32)
                for k in range(slots):
                    keep = jnp.where(live(k) == t * n_src + s, 1.0, 0.0).astype(F32)
                    block = block + adj[k].astype(F32) * keep
                dense[s, pl.ds(t * tile, tile), :] = block.astype(BF16)

    for h in range(halves):
        for d in range(1, n_z):
            block = piece(h, back(z, d, n_z), y)
            z_copy(h, d, block).wait_recv()
            for e in range(1, n_y):
                y_copy(h, e, d, block).start()

    def row_copy(h, d):
        return pltpu.make_async_remote_copy(
            src_ref=stage.at[h, d - 1], dst_ref=parts.at[h, d - 1],
            send_sem=row_send.at[h, d - 1], recv_sem=row_recv.at[h, d - 1],
            device_id=row_peer(d), device_id_type=MESH,
        )

    def block_of(h, r):
        return total[h, pl.ds(pl.multiple_of(r * rows, rows), rows), :]

    for h in range(halves):
        product = None
        for d in range(n_z):
            z_from = back(z, d, n_z)
            for e in range(1, n_y):
                y_copy(h, e, d, piece(h, z_from, back(y, e, n_y))).wait_recv()
            if small:
                values = feats[h, pl.ds(pl.multiple_of(z_from * tile, tile), tile), :]
                term = jnp.dot(dense[z_from], values, preferred_element_type=F32)
                product = term if d == 0 else product + term
        if small:
            total[h] = product
        else:
            total[h] = jnp.zeros(total.shape[1:], F32)

            def add_slot(k, carry):
                at = live(k)
                source = jnp.where(at < 0, 0, lax.rem(at, n_src))
                values = feats[h, pl.ds(pl.multiple_of(source * tile, tile), tile), :]
                term = jnp.dot(adj[k], values, preferred_element_type=F32)
                for t in range(n_tgt):
                    own = jnp.logical_and(at >= t * n_src, at < (t + 1) * n_src)
                    total[h, pl.ds(t * tile, tile), :] += term * jnp.where(own, 1.0, 0.0).astype(F32)
                return carry

            lax.fori_loop(0, slots, add_slot, 0)
        for d in row_order:
            stage[h, d - 1] = block_of(h, lax.rem(row + d, n_row)).astype(stage.dtype)
            row_copy(h, d).start()

    weight_copy.wait()
    mixed = None
    for h in range(halves):
        hidden = block_of(h, row)
        for d in reversed(row_order):
            row_copy(h, d).wait_recv()
            hidden = hidden + parts[h, d - 1].astype(F32)
        term = jnp.dot(
            hidden.astype(BF16), weight[pl.ds(h * width, width), :], preferred_element_type=F32
        )
        mixed = term if h == 0 else mixed + term
    out_ref[...] = jnp.maximum(mixed, 0.0).astype(out_ref.dtype)

    for h in range(halves):
        for d in range(1, n_z):
            z_copy(h, d, piece(h, z, y)).wait_send()
        for d in range(n_z):
            for e in range(1, n_y):
                y_copy(h, e, d, piece(h, back(z, d, n_z), y)).wait_send()
        for d in range(1, n_row):
            row_copy(h, d).wait_send()


def pair_kernel(
    n_row, n_col,
    x_ref, adj_ref, coord_ref, count_ref, w_ref, out_ref,
    own, feats, adj, weight, coord, code, dense, total, stage, parts,
    coord_sem, own_sems, adj_sem, weight_sem,
    pair_send, pair_recv, col_send, col_recv, row_send, row_recv,
):
    row, col = lax.axis_index("row"), lax.axis_index("col")
    side = col % 2
    pair = col + 1 - 2 * side
    slots, tile = adj_ref.shape[2], adj_ref.shape[3]
    rows, half = x_ref.shape[0], feats.shape[1]
    n_tgt, n_src = n_row * rows // tile, n_col * rows // tile
    targets = n_tgt * tile

    def piece(c):
        return feats.at[pl.ds(pl.multiple_of(c * rows, rows), rows)]

    def columns(h):
        return x_ref.at[:, pl.ds(pl.multiple_of(h * half, half), half)]

    coord_copy = pltpu.make_async_copy(coord_ref, coord, coord_sem)
    adj_copy = pltpu.make_async_copy(adj_ref.at[0, 0], adj.at[0], adj_sem)
    weight_copy = pltpu.make_async_copy(w_ref, weight, weight_sem)
    own_copies = [pltpu.make_async_copy(columns(h), own.at[h], own_sems.at[h]) for h in range(2)]
    own_copies.append(pltpu.make_async_copy(columns(side), piece(col), own_sems.at[2]))
    row_peers = [(e, d) for d in range(n_row) for e in range(2) if e + d > 0]
    row_peers.sort(key=lambda ed: (ed[1] % 2, -ed[1]))

    def row_peer(e, d):
        return {"row": lax.rem(row + d, n_row), "col": pair if e else col}

    barrier = pltpu.get_barrier_semaphore()
    peers = [{"col": lax.rem(col + d, n_col)} for d in range(1, n_col)]
    peers += [row_peer(e, d) for e, d in row_peers if d > 0]
    for peer in peers:
        pl.semaphore_signal(barrier, inc=1, device_id=peer, device_id_type=MESH)
    for copy in own_copies + [coord_copy, adj_copy, weight_copy]:
        copy.start()
    pl.semaphore_wait(barrier, len(peers))

    pair_adj = pltpu.make_async_remote_copy(
        src_ref=adj_ref.at[0, 0], dst_ref=adj.at[1], send_sem=pair_send.at[0],
        recv_sem=pair_recv.at[0], device_id={"col": pair}, device_id_type=MESH,
    )
    pair_adj.start()
    for copy in own_copies:
        copy.wait()

    def col_copy(d):
        return pltpu.make_async_remote_copy(
            src_ref=own.at[lax.rem(side + d, 2)], dst_ref=piece(col), send_sem=col_send.at[d],
            recv_sem=col_recv.at[col], device_id={"col": lax.rem(col + d, n_col)},
            device_id_type=MESH,
        )

    for d in range(1, n_col):
        col_copy(d).start()

    coord_copy.wait()
    for k in range(slots):
        at = jnp.where(k < count_ref[0, 0], coord[0, 0, k], -1)
        code[0, pl.ds(k, 1), :] = jnp.full((1, tile), at, jnp.int32)
    pair_code = pltpu.make_async_remote_copy(
        src_ref=code.at[0], dst_ref=code.at[1], send_sem=pair_send.at[1],
        recv_sem=pair_recv.at[1], device_id={"col": pair}, device_id_type=MESH,
    )
    pair_code.start()

    def spread(e):
        for s in range(n_src):
            for t in range(n_tgt):
                block = jnp.zeros((tile, tile), F32)
                for k in range(slots):
                    keep = jnp.where(code[e, pl.ds(k, 1), :] == t * n_src + s, 1.0, 0.0).astype(F32)
                    block = block + adj[e, k].astype(F32) * keep
                dense[s, pl.ds(e * targets + t * tile, tile), :] = block.astype(BF16)

    adj_copy.wait()
    spread(0)
    pair_adj.wait_recv()
    pair_code.wait_recv()
    spread(1)

    def arrived(c):
        pltpu.make_async_remote_copy(
            src_ref=own.at[0], dst_ref=piece(c), send_sem=col_send.at[0],
            recv_sem=col_recv.at[c], device_id={"col": pair}, device_id_type=MESH,
        ).wait_recv()

    def row_copy(e, d):
        return pltpu.make_async_remote_copy(
            src_ref=stage.at[e, d], dst_ref=parts.at[e, d], send_sem=row_send.at[e, d],
            recv_sem=row_recv.at[e, d], device_id=row_peer(e, d), device_id_type=MESH,
        )

    def block_of(e, r):
        return total[pl.ds(pl.multiple_of(e * targets + r * rows, rows), rows), :]

    for side_of in (1, 0):
        product = None
        for q in range(n_src):
            s = lax.rem(col // 2 + q, n_src)
            if side_of == 1 and q == 0:
                arrived(pair)
            elif side_of == 1:
                arrived(2 * s)
                arrived(2 * s + 1)
            values = feats[pl.ds(pl.multiple_of(s * tile, tile), tile), :]
            tiles = dense[s, pl.ds(side_of * targets, targets), :]
            term = jnp.dot(tiles, values, preferred_element_type=F32)
            product = term if q == 0 else product + term
        total[pl.ds(side_of * targets, targets), :] = product
        for e, d in row_peers:
            if e == side_of:
                stage[e, d] = block_of(e, lax.rem(row + d, n_row)).astype(stage.dtype)
                row_copy(e, d).start()
    weight_copy.wait()
    hidden = [block_of(0, row), jnp.zeros((rows, half), F32)]
    for e, d in reversed(row_peers):
        row_copy(e, d).wait_recv()
        hidden[e] = hidden[e] + parts[e, d].astype(F32)

    def weight_rows(h):
        return weight[pl.ds(pl.multiple_of(h * half, half), half), :]

    mixed = jnp.dot(hidden[0].astype(BF16), weight_rows(side), preferred_element_type=F32)
    mixed += jnp.dot(hidden[1].astype(BF16), weight_rows(1 - side), preferred_element_type=F32)
    out_ref[...] = jnp.maximum(mixed, 0.0).astype(out_ref.dtype)

    pair_adj.wait_send()
    pair_code.wait_send()
    for d in range(1, n_col):
        col_copy(d).wait_send()
    for e, d in row_peers:
        row_copy(e, d).wait_send()


def hbm(array):
    return pltpu.with_memory_space_constraint(array, pltpu.HBM)


def pair_call(n_row, n_col, features, adj_tiles, tile_coord, tile_count, weight):
    rows, width = features.shape
    slots, tile = adj_tiles.shape[2:4]
    targets, n_src, half = n_row * rows, n_col * rows // tile, width // 2
    dma = pltpu.SemaphoreType.DMA
    in_hbm = pl.BlockSpec(memory_space=pltpu.HBM)
    return pl.pallas_call(
        functools.partial(pair_kernel, n_row, n_col),
        out_shape=jax.ShapeDtypeStruct((rows, weight.shape[1]), BF16),
        in_specs=[in_hbm, in_hbm, in_hbm, pl.BlockSpec(memory_space=pltpu.SMEM), in_hbm],
        out_specs=pl.BlockSpec(memory_space=pltpu.VMEM),
        scratch_shapes=[
            pltpu.VMEM((2, rows, half), BF16),
            pltpu.VMEM((n_col * rows, half), BF16),
            pltpu.VMEM((2, slots, tile, tile), BF16),
            pltpu.VMEM(weight.shape, BF16),
            pltpu.SMEM(tile_coord.shape, jnp.int32),
            pltpu.VMEM((2, 8, tile), jnp.int32),
            pltpu.VMEM((n_src, 2 * targets, tile), BF16),
            pltpu.VMEM((2 * targets, half), F32),
            pltpu.VMEM((2, n_row, rows, half), BF16),
            pltpu.VMEM((2, n_row, rows, half), BF16),
            dma, dma((3,)), dma, dma,
            dma((2,)), dma((2,)),
            dma((n_col,)), dma((n_col,)),
            dma((2, n_row)), dma((2, n_row)),
        ],
        compiler_params=pltpu.CompilerParams(
            collective_id=0, has_side_effects=True, vmem_limit_bytes=32 * 2**20
        ),
    )(hbm(features), hbm(adj_tiles), hbm(tile_coord), tile_count, hbm(weight))


def solution(mesh):
    n_row, n_col = mesh.shape["row"], mesh.shape["col"]
    n_y = max(1, n_row // 2)
    if n_col % n_y:
        n_y = 1
    n_z = n_col // n_y

    def on_device(features, adj_tiles, tile_coord, tile_count, weight):
        rows, width = features.shape
        slots, tile = adj_tiles.shape[2:4]
        n_tgt = n_row * rows // tile
        n_src = n_col * rows // tile
        paired = slots <= 8 and 2 * rows == tile and width == 2 * tile and n_col % 2 == 0
        if paired:
            return pair_call(n_row, n_col, features, adj_tiles, tile_coord, tile_count, weight)
        small = slots <= 8 and n_y * rows == tile
        in_hbm = pl.BlockSpec(memory_space=pltpu.HBM)
        dma = pltpu.SemaphoreType.DMA
        halves = 2
        half = width // halves
        return pl.pallas_call(
            functools.partial(kernel, n_row, n_z, n_y),
            out_shape=jax.ShapeDtypeStruct((rows, weight.shape[1]), BF16),
            in_specs=[in_hbm] * 5,
            out_specs=pl.BlockSpec(memory_space=pltpu.VMEM),
            scratch_shapes=[
                pltpu.VMEM((halves, n_col * rows, half), BF16),
                pltpu.VMEM((slots, tile, tile), BF16),
                pltpu.VMEM(weight.shape, BF16),
                pltpu.SMEM(tile_coord.shape, jnp.int32),
                pltpu.SMEM(tile_count.shape, jnp.int32),
                pltpu.VMEM((n_src, n_tgt * tile, tile) if small else (1, 16, 128), BF16),
                pltpu.VMEM((halves, n_tgt * tile, half), F32),
                pltpu.VMEM((halves, n_row - 1, rows, half), BF16),
                pltpu.VMEM((halves, n_row - 1, rows, half), BF16),
                dma((2,)), dma((halves,)), dma, dma,
                dma((halves, n_z)), dma((halves, n_z)),
                dma((halves, n_y, n_z)), dma((halves, n_y, n_z)),
                dma((halves, n_row - 1)), dma((halves, n_row - 1)),
            ],
            compiler_params=pltpu.CompilerParams(
                collective_id=0, has_side_effects=True, vmem_limit_bytes=32 * 2**20
            ),
        )(hbm(features), hbm(adj_tiles), hbm(tile_coord), tile_count, hbm(weight))

    return jax.shard_map(
        on_device,
        mesh=mesh,
        in_specs=(
            P(("row", "col"), None),
            P("row", "col", None, None, None),
            P("row", "col", None),
            P("row", "col"),
            P(),
        ),
        out_specs=P(("col", "row"), None),
        check_vma=False,
    )
```
